32 devices in a mesh: row: 16 (over z, y, core), col: 2 (over x).
Axes of the slice: x: 2, y: 2, z: 4, core: 2. Of those that a mesh axis runs over, the one named last changes fastest.
Arguments:
- pair_prefactor: bfloat16 [4, 10240, 10240], P(None, 'row', 'col'), may hold values from -6 to 6
- boys_argument: bfloat16 [4, 10240, 10240], P(None, 'row', 'col'), may hold values from 1 to 4
- orbitals: bfloat16 [10240, 1024], P('col', 'row'), may hold values from -0.0625 to 0.0625
- screen_mask: int32 [80, 80], replicated, may hold values 0 or 1
- momentum: int32 [80], replicated, may hold values from 0 to 3
Outputs:
- exchange_matrix: float32 [10240, 10240], P('row', 'col')
The draws below stay inside these ranges and needn't reach their ends.
Inputs may be any that keep to these rules, and one draw needn't show every extreme that they name: `screen_mask`: 1 where the block pair passes screening, else 0. One angular momentum for each block of 128 basis functions.
All inputs are finite; a program needn't handle non-finite values.
Results may differ from the reference program's by a relative error of at most 0.0047.
Values may be sent and summed in bfloat16 or wider, within the bound.
A program may use at most 192 MiB of HBM per device.

```python
import math
import jax
import jax.numpy as jnp
from jax import lax

N = 10240
NOCC = 1024
BLK = 128
MAXL = 3
AUX = 4
NBLK = 80


def place_ends(values, stream_key, smallest, high):
    spot = [jax.random.randint(jax.random.fold_in(stream_key, axis), (), 0, length) for axis, length in enumerate(values.shape)]
    longest = values.shape.index(max(values.shape))
    neighbour = spot[:longest] + [(spot[longest] + 1) % values.shape[longest]] + spot[longest + 1:]
    return values.at[tuple(spot)].set(smallest).at[tuple(neighbour)].set(high)


def steps_of(own_key, extent, split, least, top_value):
    def one(axis_at, blocks):
        heights = jax.random.uniform(jax.random.fold_in(jax.random.fold_in(own_key, 6), axis_at), (blocks,), jnp.float32, least / len(split), top_value / len(split))
        return jnp.repeat(jnp.exp(heights), extent[axis_at] // blocks).reshape((-1,) + (1,) * (len(extent) - axis_at - 1))

    factor_of = one(*split[0])
    for cut in split[1:]:
        factor_of = factor_of * one(*cut)
    return factor_of


def normal_values(rng, shape, spread, limit, shards=(), kind=jnp.bfloat16):
    array = spread * jax.random.normal(rng, shape, jnp.float32)
    if shards:
        array = array * steps_of(rng, shape, shards, -0.22, 0.18)
    return jnp.clip(array, -limit, limit).astype(kind)


def setup_inputs(seed: int = 0) -> dict:
    key_of = jax.random.split(jax.random.key(seed), 6)
    return {
        "pair_prefactor": normal_values(key_of[0], (AUX, N, N), 1.0, 6.0, ((1, 16), (2, 2))),
        "boys_argument": jnp.clip(jnp.exp(math.log(4.0) - 1.3862944 * jax.random.uniform(key_of[1], (AUX, N, N), jnp.float32) ** steps_of(key_of[1], (AUX, N, N), ((1, 16), (2, 2)), -0.2, 0.2)), 1.0, 4.0).astype(jnp.bfloat16),
        "orbitals": normal_values(key_of[2], (N, NOCC), N ** -0.5, 0.0625, ((0, 2), (1, 16))),
        "screen_mask": place_ends((jax.random.randint(key_of[3], (NBLK, NBLK), 0, 4) < 3).astype(jnp.int32), jax.random.fold_in(key_of[3], 1), 0, 1),
        "momentum": place_ends(jax.random.randint(key_of[4], (NBLK,), 0, MAXL + 1), jax.random.fold_in(key_of[4], 1), 0, MAXL).astype(jnp.int32),
    }


def boys_value(argument, order):
    decay = jnp.exp(-argument)
    current = 0.5 * jnp.sqrt(jnp.pi / argument) * jax.scipy.special.erf(jnp.sqrt(argument))
    chosen = jnp.where(order == 0, current, jnp.zeros_like(current))
    for level in range(2 * MAXL):
        current = ((2.0 * level + 1.0) * current - decay) / (2.0 * argument)
        chosen = jnp.where(order == level + 1, current, chosen)
    return chosen

def tile_values(prefactor, argument, order, screen):
    argument_full = argument.astype(jnp.float32)
    factor = (2 * order + 1).astype(jnp.float32) * boys_value(argument_full, order)
    return (prefactor.astype(jnp.float32) * factor * screen).astype(jnp.bfloat16)

def reference(pair_prefactor, boys_argument, orbitals, screen_mask, momentum):
    per_function = jnp.repeat(momentum, BLK)
    order_sum = per_function[:, None] + per_function[None, :]
    screen_full = jnp.repeat(jnp.repeat(screen_mask, BLK, axis=0), BLK, axis=1).astype(jnp.float32)

    def half_one(pair):
        prefactor, argument = pair
        tile_vals = tile_values(prefactor, argument, order_sum, screen_full)
        return jnp.dot(tile_vals, orbitals, preferred_element_type=jnp.float32).astype(jnp.bfloat16)
    half_panel = lax.map(half_one, (pair_prefactor, boys_argument))
    result = jnp.zeros((N, N), jnp.float32)
    for index in range(AUX):
        result = result + jnp.dot(half_panel[index], half_panel[index].T, preferred_element_type=jnp.float32)
    return result * (1.0 / math.sqrt(AUX * NOCC))
```

```python
import functools
import math

import jax
import jax.numpy as jnp
from jax import lax
from jax.experimental import pallas as pl
from jax.experimental.pallas import tpu as pltpu
from jax.sharding import PartitionSpec as P

NOCC = 1024
BLK = 128
AUX = 4
CHUNKS = 5
SUB = 64


def tile_kernel(first, order_ref, screen_ref, pre_ref, arg_ref, out_ref):
    span = pre_ref.shape[2] // BLK
    row = first + pl.program_id(0)
    start = pl.program_id(1) * span

    for p in range(pre_ref.shape[0]):
        for b in range(span):
            order = order_ref[row, start + b]
            cols = pl.ds(b * BLK, BLK)

            @pl.when(screen_ref[row, start + b] == 0)
            def _():
                out_ref[p, :, cols] = jnp.zeros((SUB, BLK), out_ref.dtype)

            @pl.when(screen_ref[row, start + b] != 0)
            def _():
                t = arg_ref[p, :, cols].astype(jnp.float32)
                decay = jnp.exp(-t)
                inverse_root = lax.rsqrt(t)
                half_inverse = 0.5 * inverse_root * inverse_root
                value = (0.5 * math.sqrt(math.pi)) * inverse_root * lax.erf(t * inverse_root)

                def step(level, value):
                    odd = (2 * level + 1).astype(jnp.float32)
                    return (odd * value - decay) * half_inverse

                value = lax.fori_loop(0, order, step, value)
                weight = (2 * order + 1).astype(jnp.float32)
                pre = pre_ref[p, :, cols].astype(jnp.float32)
                out_ref[p, :, cols] = (pre * (weight * value)).astype(out_ref.dtype)


def tile_chunk(pair_prefactor, boys_argument, order, screen, chunk, height):
    aux, _, width = pair_prefactor.shape
    first = chunk * height // SUB
    wide = width // 2
    spec = pl.BlockSpec((aux, SUB, wide), lambda i, j, *_: (0, first + i, j))
    return pl.pallas_call(
        functools.partial(tile_kernel, first),
        out_shape=jax.ShapeDtypeStruct((aux, height, width), jnp.bfloat16),
        grid_spec=pltpu.PrefetchScalarGridSpec(
            num_scalar_prefetch=2,
            grid=(height // SUB, width // wide),
            in_specs=[spec, spec],
            out_specs=pl.BlockSpec((aux, SUB, wide), lambda i, j, *_: (0, i, j)),
        ),
        compiler_params=pltpu.CompilerParams(vmem_limit_bytes=32 << 20),
        cost_estimate=pl.CostEstimate(
            flops=60 * aux * height * width,
            bytes_accessed=6 * aux * height * width,
            transcendentals=3 * aux * height * width,
        ),
    )(order, screen, pair_prefactor, boys_argument)


def assemble_kernel(height, per, scale, *refs):
    own, received, out_ref = refs[:CHUNKS], refs[CHUNKS:-1], refs[-1]
    extra = len(received) // CHUNKS
    for chunk in range(CHUNKS):
        total = own[chunk][...]
        for part in received[chunk * extra : (chunk + 1) * extra]:
            total = total + part[...].astype(jnp.float32)
        total = total * scale
        for s in range(per):
            at = s * CHUNKS * height + chunk * height
            out_ref[:, at : at + height] = total[:, s * height : (s + 1) * height]


def assemble(own, received, height, per, scale):
    rows, span = own[0].shape
    spec = pl.BlockSpec((SUB, span), lambda i: (i, 0))
    return pl.pallas_call(
        functools.partial(assemble_kernel, height, per, scale),
        out_shape=jax.ShapeDtypeStruct((rows, CHUNKS * span), jnp.float32),
        grid=(rows // SUB,),
        in_specs=[spec] * (len(own) + len(received)),
        out_specs=pl.BlockSpec((SUB, CHUNKS * span), lambda i: (i, 0)),
        compiler_params=pltpu.CompilerParams(vmem_limit_bytes=32 << 20),
    )(*own, *received)


def body(cols, pair_prefactor, boys_argument, orbitals, screen_mask, momentum):
    mine_rows, mine_cols = pair_prefactor.shape[1:]
    row_index = lax.axis_index("row")
    col_index = lax.axis_index("col")
    height = mine_rows // CHUNKS
    share = NOCC // cols
    per = mine_cols // mine_rows
    span = per * height
    scale = 1.0 / math.sqrt(AUX * NOCC)

    coeff_all = lax.all_gather(orbitals, "row", axis=1, tiled=True)

    row_blocks = (row_index * mine_rows + SUB * lax.iota(jnp.int32, mine_rows // SUB)) // BLK
    col_blocks = col_index * (mine_cols // BLK) + lax.iota(jnp.int32, mine_cols // BLK)
    order = momentum[row_blocks][:, None] + momentum[col_blocks][None, :]
    screen = screen_mask[row_blocks][:, col_blocks]

    peers = [lax.rem(col_index + k, cols) for k in range(cols)]
    coeff = [lax.dynamic_slice_in_dim(coeff_all, peer * share, share, 1) for peer in peers]
    paths = [[(i, (i + k) % cols) for i in range(cols)] for k in range(cols)]

    def project(tile, part):
        return jnp.einsum("pmn,nk->pmk", tile, part, preferred_element_type=jnp.float32)

    shares, panels, tiles = [], [], []
    for chunk in range(CHUNKS):
        if chunk >= 2:
            order = lax.optimization_barrier((order, shares[chunk - 2]))[0]
        tiles.append(tile_chunk(pair_prefactor, boys_argument, order, screen, chunk, height))
        tile = tiles[-1]
        if chunk >= 1:
            tile = lax.optimization_barrier((tile, shares[chunk - 1]))[0]
        received = [
            lax.ppermute(project(tile, coeff[k]).astype(jnp.bfloat16), "col", paths[k])
            for k in range(1, cols)
        ]
        total = lax.optimization_barrier(project(tile, coeff[0]))
        for part in received:
            total = total + part.astype(jnp.float32)
        shares.append(total.astype(jnp.bfloat16))
        panels.append(lax.all_gather(shares[-1], "row", axis=1, tiled=True))

    mine = jnp.concatenate(shares, axis=1)

    def product(panel, peer):
        other = lax.dynamic_slice_in_dim(panel, peer * span, span, 1)
        return jnp.einsum("pmk,pnk->mn", mine, other, preferred_element_type=jnp.float32)

    own, received = [], []
    for chunk, panel in enumerate(panels):
        if chunk:
            panel = lax.optimization_barrier((panel, own[-1]))[0]
        received += [
            lax.ppermute(product(panel, peers[k]).astype(jnp.bfloat16), "col", paths[k])
            for k in range(1, cols)
        ]
        own.append(lax.optimization_barrier(product(panel, peers[0])))
    return assemble(own, received, height, per, scale)


def solution(mesh):
    placed = (P(None, "row", "col"), P(None, "row", "col"), P("col", "row"), P(), P())
    return jax.shard_map(
        functools.partial(body, mesh.shape["col"]),
        mesh=mesh, in_specs=placed, out_specs=P("row", "col"), check_vma=False,
    )
```

```python
import functools
import math

import jax
import jax.numpy as jnp
from jax import lax
from jax.experimental import pallas as pl
from jax.experimental.pallas import tpu as pltpu
from jax.sharding import PartitionSpec as P

NOCC = 1024
BLK = 128
AUX = 4
PIECES = (3, 2)
CHUNKS = len(PIECES)
SUB = 64


def tile_kernel(first, order_ref, screen_ref, pre_ref, arg_ref, out_ref):
    span = pre_ref.shape[2] // BLK
    row = first + pl.program_id(0)
    start = pl.program_id(1) * span

    for p in range(pre_ref.shape[0]):
        for b in range(span):
            order = order_ref[row, start + b]
            cols = pl.ds(b * BLK, BLK)

            @pl.when(screen_ref[row, start + b] == 0)
            def _():
                out_ref[p, :, cols] = jnp.zeros((SUB, BLK), out_ref.dtype)

            @pl.when(screen_ref[row, start + b] != 0)
            def _():
                t = arg_ref[p, :, cols].astype(jnp.float32)
                decay = jnp.exp(-t)
                inverse_root = lax.rsqrt(t)
                half_inverse = 0.5 * inverse_root * inverse_root
                value = (0.5 * math.sqrt(math.pi)) * inverse_root * lax.erf(t * inverse_root)

                def step(level, value):
                    odd = (2 * level + 1).astype(jnp.float32)
                    return (odd * value - decay) * half_inverse

                value = lax.fori_loop(0, order, step, value)
                weight = (2 * order + 1).astype(jnp.float32)
                pre = pre_ref[p, :, cols].astype(jnp.float32)
                out_ref[p, :, cols] = (pre * (weight * value)).astype(out_ref.dtype)


def tile_chunk(pair_prefactor, boys_argument, order, screen, start, height):
    aux, _, width = pair_prefactor.shape
    first = start // SUB
    wide = width // 2
    spec = pl.BlockSpec((aux, SUB, wide), lambda i, j, *_: (0, first + i, j))
    return pl.pallas_call(
        functools.partial(tile_kernel, first),
        out_shape=jax.ShapeDtypeStruct((aux, height, width), jnp.bfloat16),
        grid_spec=pltpu.PrefetchScalarGridSpec(
            num_scalar_prefetch=2,
            grid=(height // SUB, width // wide),
            in_specs=[spec, spec],
            out_specs=pl.BlockSpec((aux, SUB, wide), lambda i, j, *_: (0, i, j)),
        ),
        compiler_params=pltpu.CompilerParams(vmem_limit_bytes=32 << 20),
        cost_estimate=pl.CostEstimate(
            flops=60 * aux * height * width,
            bytes_accessed=6 * aux * height * width,
            transcendentals=3 * aux * height * width,
        ),
    )(order, screen, pair_prefactor, boys_argument)


def assemble_kernel(heights, starts, per, scale, *refs):
    own, received, out_ref = refs[:CHUNKS], refs[CHUNKS:-1], refs[-1]
    extra = len(received) // CHUNKS
    for chunk in range(CHUNKS):
        total = own[chunk][...]
        for part in received[chunk * extra : (chunk + 1) * extra]:
            total = total + part[...].astype(jnp.float32)
        total = total * scale
        for s in range(per):
            height = heights[chunk]
            at = s * sum(heights) + starts[chunk]
            out_ref[:, at : at + height] = total[:, s * height : (s + 1) * height]


def assemble(own, received, heights, starts, per, scale):
    rows = own[0].shape[0]
    width = per * sum(heights)
    spec = lambda a: pl.BlockSpec((SUB, a.shape[1]), lambda i: (i, 0))
    return pl.pallas_call(
        functools.partial(assemble_kernel, heights, starts, per, scale),
        out_shape=jax.ShapeDtypeStruct((rows, width), jnp.float32),
        grid=(rows // SUB,),
        in_specs=[spec(a) for a in own + received],
        out_specs=pl.BlockSpec((SUB, width), lambda i: (i, 0)),
        compiler_params=pltpu.CompilerParams(vmem_limit_bytes=32 << 20),
    )(*own, *received)


def body(cols, pair_prefactor, boys_argument, orbitals, screen_mask, momentum):
    mine_rows, mine_cols = pair_prefactor.shape[1:]
    row_index = lax.axis_index("row")
    col_index = lax.axis_index("col")
    heights = [mine_rows * piece // sum(PIECES) for piece in PIECES]
    starts = [sum(heights[:i]) for i in range(CHUNKS)]
    share = NOCC // cols
    per = mine_cols // mine_rows
    scale = 1.0 / math.sqrt(AUX * NOCC)

    coeff_all = lax.all_gather(orbitals, "row", axis=1, tiled=True)

    row_blocks = (row_index * mine_rows + SUB * lax.iota(jnp.int32, mine_rows // SUB)) // BLK
    col_blocks = col_index * (mine_cols // BLK) + lax.iota(jnp.int32, mine_cols // BLK)
    order = momentum[row_blocks][:, None] + momentum[col_blocks][None, :]
    screen = screen_mask[row_blocks][:, col_blocks]

    peers = [lax.rem(col_index + k, cols) for k in range(cols)]
    coeff = [lax.dynamic_slice_in_dim(coeff_all, peer * share, share, 1) for peer in peers]
    paths = [[(i, (i + k) % cols) for i in range(cols)] for k in range(cols)]

    def project(tile, part):
        return jnp.einsum("pmn,nk->pmk", tile, part, preferred_element_type=jnp.float32)

    shares, panels, tiles = [], [], []
    for chunk in range(CHUNKS):
        if chunk >= 2:
            order = lax.optimization_barrier((order, shares[chunk - 2]))[0]
        tiles.append(tile_chunk(pair_prefactor, boys_argument, order, screen, starts[chunk], heights[chunk]))
        tile = tiles[-1]
        if chunk >= 1:
            tile = lax.optimization_barrier((tile, shares[chunk - 1]))[0]
        received = [
            lax.ppermute(project(tile, coeff[k]).astype(jnp.bfloat16), "col", paths[k])
            for k in range(1, cols)
        ]
        total = lax.optimization_barrier(project(tile, coeff[0]))
        for part in received:
            total = total + part.astype(jnp.float32)
        total = total.astype(jnp.bfloat16)
        shares.append(jnp.concatenate([total[p] for p in range(AUX)], axis=1))
        panels.append(lax.all_gather(shares[-1], "row", axis=0, tiled=True))

    mine = jnp.concatenate(shares, axis=0)

    def product(panel, peer):
        span = panel.shape[0] // cols
        other = lax.dynamic_slice_in_dim(panel, peer * span, span, 0)
        return jnp.einsum("mk,nk->mn", mine, other, preferred_element_type=jnp.float32)

    own, received = [], []
    for chunk, panel in enumerate(panels):
        if chunk:
            panel = lax.optimization_barrier((panel, own[-1]))[0]
        received += [
            lax.ppermute(product(panel, peers[k]).astype(jnp.bfloat16), "col", paths[k])
            for k in range(1, cols)
        ]
        own.append(lax.optimization_barrier(product(panel, peers[0])))
    return assemble(own, received, heights, starts, per, scale)


def solution(mesh):
    placed = (P(None, "row", "col"), P(None, "row", "col"), P("col", "row"), P(), P())
    return jax.shard_map(
        functools.partial(body, mesh.shape["col"]),
        mesh=mesh, in_specs=placed, out_specs=P("row", "col"), check_vma=False,
    )
```
